512 devices in a mesh: row: 16 (over z, core), col: 32 (over x, y).
Axes of the slice: x: 4, y: 8, z: 8, core: 2. Of those that a mesh axis runs over, the one named last changes fastest.
Arguments:
- activations: bfloat16 [512, 12288], P('col', 'row'), may hold values from -6 to 6
- in_weight: bfloat16 [12288, 24576], P('row', 'col'), may hold values from -0.0546875 to 0.0546875
- out_weight: bfloat16 [24576, 12288], P('col', 'row'), may hold values from -0.0390625 to 0.0390625
- cotangent: bfloat16 [512, 12288], P('col', 'row'), may hold values from -2 to 2
Outputs:
- layer_output: bfloat16 [512, 12288], P('col', 'row')
- input_gradient: bfloat16 [512, 12288], P('col', 'row')
- in_weight_gradient: bfloat16 [12288, 24576], P('row', 'col')
- out_weight_gradient: bfloat16 [24576, 12288], P('col', 'row')
The draws below stay inside these ranges and needn't reach their ends.
All inputs are finite; a program needn't handle non-finite values.
Results may differ from the reference program's by a relative error of at most 0.035.
Values may be sent and summed in bfloat16 or wider, within the bound.
No kernel may reach another device: no remote copies, remote signals or barrier semaphores. Data moves between devices by JAX's collectives and lax.ppermute only.
A program may use at most 64 MiB of HBM per device.

```python
import math
import jax
import jax.numpy as jnp
from jax import lax

D = 12288
FF = 24576
TOKENS = 512
N_ROW = 16
N_COL = 32


def block_levels(stream_key, shape, shards, smallest, top_value):
    def one(dim, blocks):
        heights = jax.random.uniform(jax.random.fold_in(jax.random.fold_in(stream_key, 6), dim), (blocks,), jnp.float32, smallest / len(shards), top_value / len(shards))
        return jnp.repeat(jnp.exp(heights), shape[dim] // blocks).reshape((-1,) + (1,) * (len(shape) - dim - 1))

    factor_of = one(*shards[0])
    for cut in shards[1:]:
        factor_of = factor_of * one(*cut)
    return factor_of


def bell_draw(key, extent, scale, most, shards=(), kind=jnp.bfloat16):
    result = scale * jax.random.normal(key, extent, jnp.float32)
    if shards:
        result = result * block_levels(key, extent, shards, -0.22, 0.18)
    return jnp.clip(result, -most, most).astype(kind)


def setup_inputs(seed: int = 0) -> dict:
    streams_of = jax.random.split(jax.random.key(seed), 5)
    activations = bell_draw(streams_of[0], (TOKENS, D), 1.0, 6.0, ((0, 32), (1, 16)))
    in_weight = bell_draw(streams_of[1], (D, FF), D ** -0.5, 0.0546875, ((0, 16), (1, 32)))
    out_weight = bell_draw(streams_of[2], (FF, D), FF ** -0.5, 0.0390625, ((0, 32), (1, 16)))
    cotangent = bell_draw(streams_of[3], (TOKENS, D), 0.3, 2.0, ((0, 32), (1, 16)))
    return dict(activations=activations, in_weight=in_weight, out_weight=out_weight, cotangent=cotangent)


GELU_C = math.sqrt(2.0 / math.pi)

def gelu_value(hidden):
    inner = GELU_C * (hidden + 0.044715 * hidden * hidden * hidden)
    return 0.5 * hidden * (1.0 + jnp.tanh(inner))

def gelu_slope(hidden):
    tanh_value = jnp.tanh(GELU_C * (hidden + 0.044715 * hidden * hidden * hidden))
    return 0.5 * (1.0 + tanh_value) + 0.5 * hidden * (1.0 - tanh_value * tanh_value) * GELU_C * (1.0 + 3.0 * 0.044715 * hidden * hidden)

def block_sum(left_side, right_side, blocks):
    width = left_side.shape[1] // blocks

    def advance(running, block_index):
        left_block = lax.dynamic_slice_in_dim(left_side, block_index * width, width, 1)
        right_block = lax.dynamic_slice_in_dim(right_side, block_index * width, width, 0)
        product = jnp.dot(left_block, right_block, preferred_element_type=jnp.float32)
        rounded = lax.optimization_barrier(product.astype(jnp.bfloat16))
        return (running + rounded.astype(jnp.float32), None)
    initial = jnp.zeros((left_side.shape[0], right_side.shape[1]), jnp.float32)
    running, unused = lax.scan(advance, initial, jnp.arange(blocks, dtype=jnp.int32))
    return running

def reference(activations, in_weight, out_weight, cotangent):
    pre_act = block_sum(activations, in_weight, N_ROW)
    hidden_act = gelu_value(pre_act).astype(jnp.bfloat16)
    layer_output = block_sum(hidden_act, out_weight, N_COL).astype(jnp.bfloat16)
    act_grad = block_sum(cotangent, out_weight.T, N_ROW)
    pre_grad = (act_grad * gelu_slope(pre_act)).astype(jnp.bfloat16)
    in_weight_gradient = jnp.dot(activations.T, pre_grad, preferred_element_type=jnp.float32).astype(jnp.bfloat16)
    out_weight_gradient = jnp.dot(hidden_act.T, cotangent, preferred_element_type=jnp.float32).astype(jnp.bfloat16)
    input_gradient = block_sum(pre_grad, in_weight.T, N_COL).astype(jnp.bfloat16)
    return (layer_output, input_gradient, in_weight_gradient, out_weight_gradient)
```

```python
import math

import jax
import jax.numpy as jnp
import numpy as np
from jax import lax
from jax.sharding import Mesh, PartitionSpec as P

GELU_C = math.sqrt(2.0 / math.pi)
BF16 = jnp.bfloat16
F32 = jnp.float32

CORES = 2
Y_NEAR = 2
Y_FAR = 4
NEAR = ("x", "yl")
FAR = ("yh", "core")


def gelu_value(hidden):
    inner = GELU_C * (hidden + 0.044715 * hidden * hidden * hidden)
    return 0.5 * hidden * (1.0 + jnp.tanh(inner))


def gelu_slope(hidden):
    tanh_value = jnp.tanh(GELU_C * (hidden + 0.044715 * hidden * hidden * hidden))
    return 0.5 * (1.0 + tanh_value) + 0.5 * hidden * (1.0 - tanh_value * tanh_value) * GELU_C * (
        1.0 + 3.0 * 0.044715 * hidden * hidden
    )


def times(left_side, right_side):
    return jnp.dot(left_side, right_side, preferred_element_type=F32)


def times_transposed(left_side, right_side):
    return lax.dot_general(
        left_side, right_side, (((1,), (1,)), ((), ())), preferred_element_type=F32
    )


def over_tokens(left_side, right_side):
    return lax.dot_general(
        left_side, right_side, (((0,), (0,)), ((), ())), preferred_element_type=F32
    )


def exchange(blocks, axes):
    return lax.all_to_all(blocks, axes, 0, 0, tiled=True)


def to_all(block, count, axes):
    return exchange(jnp.broadcast_to(block[None], (count,) + block.shape), axes)


def swap_cores(block):
    return lax.ppermute(block, "core", [(0, 1), (1, 0)])


def shards(n_z, n_near, n_far, activations, in_weight, out_weight, cotangent):
    tokens, width = activations.shape
    half = tokens // CORES
    core = lax.axis_index("core")

    in_pair = lax.all_gather(in_weight, "core", axis=0, tiled=True)
    out_pair = lax.all_gather(out_weight, "core", axis=1, tiled=True)

    sent = jnp.stack([activations, cotangent]).reshape(2, CORES, half, width)
    sent = jnp.broadcast_to(sent.transpose(1, 0, 2, 3)[None], (n_far, CORES, 2, half, width))
    got = exchange(sent.reshape(n_far * CORES, 2, half, width), FAR)
    got = got.reshape(n_far, CORES, 2, half, width).transpose(2, 0, 3, 1, 4)
    got = to_all(got.reshape(2, n_far * half, CORES * width), n_near, NEAR)
    some = n_near * n_far * half
    token_inputs = got[:, 0].reshape(some, CORES * width)
    token_cotangent = got[:, 1].reshape(some, CORES * width)

    pre_part = times(token_inputs, in_pair).astype(BF16)
    act_part = times_transposed(token_cotangent, out_pair).astype(BF16)
    hidden = pre_part.shape[1]
    few = some // n_z
    parts = jnp.stack([pre_part.reshape(n_z, few, hidden), act_part.reshape(n_z, few, hidden)], 1)
    sums = jnp.sum(exchange(parts, "z").astype(F32), axis=0)
    pre_act, act_grad = sums[0], sums[1]
    hidden_rows = gelu_value(pre_act).astype(BF16)
    pre_grad_rows = (act_grad * gelu_slope(pre_act)).astype(BF16)
    rows = to_all(jnp.stack([hidden_rows, pre_grad_rows]), n_z, "z")
    hidden_act = rows[:, 0].reshape(some, hidden)
    pre_grad = rows[:, 1].reshape(some, hidden)

    out_part = times(hidden_act, out_pair).astype(BF16)
    in_part = times_transposed(pre_grad, in_pair).astype(BF16)
    shape = (n_near, n_far * half, CORES * width)
    parts = jnp.stack([out_part.reshape(shape), in_part.reshape(shape)], 1)
    sums = jnp.sum(exchange(parts, NEAR).astype(F32), axis=0).astype(BF16)
    parts = sums.reshape(2, n_far, half, CORES, width).transpose(1, 3, 0, 2, 4)
    parts = exchange(parts.reshape(n_far * CORES, 2, half, width), FAR)
    sums = jnp.sum(parts.reshape(n_far, CORES, 2, half, width).astype(F32), axis=0).astype(BF16)
    sums = sums.transpose(1, 0, 2, 3).reshape(2, tokens, width)

    def own_and_other(block):
        own = lax.dynamic_slice_in_dim(block, core * width, width, 1)
        other = lax.dynamic_slice_in_dim(block, (1 - core) * width, width, 1)
        return own, swap_cores(other)

    inputs_own, inputs_other = own_and_other(token_inputs)
    cotangent_own, cotangent_other = own_and_other(token_cotangent)
    hidden_other = swap_cores(hidden_act)
    pre_grad_other = swap_cores(pre_grad)
    in_weight_gradient = (
        over_tokens(inputs_own, pre_grad) + over_tokens(inputs_other, pre_grad_other)
    ).astype(BF16)
    out_weight_gradient = (
        over_tokens(hidden_act, cotangent_own) + over_tokens(hidden_other, cotangent_other)
    ).astype(BF16)
    return sums[0], sums[1], in_weight_gradient, out_weight_gradient


def solution(mesh):
    n_z = mesh.shape["row"] // CORES
    n_x = mesh.shape["col"] // (Y_NEAR * Y_FAR)
    fine = Mesh(
        np.asarray(mesh.devices).reshape(n_z, CORES, n_x, Y_FAR, Y_NEAR),
        ("z", "core", "x", "yh", "yl"),
    )
    row, col = ("z", "core"), ("x", "yh", "yl")

    def part(*arrays):
        return shards(n_z, n_x * Y_NEAR, Y_FAR, *arrays)

    return jax.shard_map(
        part,
        mesh=fine,
        in_specs=(P(col, row), P(row, col), P(col, row), P(col, row)),
        out_specs=(P(col, row), P(col, row), P(row, col), P(col, row)),
        check_vma=False,
    )
```

```python
import math

import jax
import jax.numpy as jnp
import numpy as np
from jax import lax
from jax.experimental import pallas as pl
from jax.experimental.pallas import tpu as pltpu
from jax.sharding import Mesh, PartitionSpec as P

GELU_C = math.sqrt(2.0 / math.pi)
BF16 = jnp.bfloat16
F32 = jnp.float32

CORES = 2
Y_NEAR = 2
Y_FAR = 4
NEAR = ("x", "yl")
FAR = ("yh", "core")


def gelu_value(hidden):
    inner = GELU_C * (hidden + 0.044715 * hidden * hidden * hidden)
    return 0.5 * hidden * (1.0 + jnp.tanh(inner))


def gelu_slope(hidden):
    tanh_value = jnp.tanh(GELU_C * (hidden + 0.044715 * hidden * hidden * hidden))
    return 0.5 * (1.0 + tanh_value) + 0.5 * hidden * (1.0 - tanh_value * tanh_value) * GELU_C * (
        1.0 + 3.0 * 0.044715 * hidden * hidden
    )


def times(left_side, right_side):
    return jnp.dot(left_side, right_side, preferred_element_type=F32)


def times_transposed(left_side, right_side):
    return lax.dot_general(
        left_side, right_side, (((1,), (1,)), ((), ())), preferred_element_type=F32
    )


def over_tokens(left_side, right_side):
    return lax.dot_general(
        left_side, right_side, (((0,), (0,)), ((), ())), preferred_element_type=F32
    )


def exchange(blocks, axes):
    return lax.all_to_all(blocks, axes, 0, 0, tiled=True)


def to_all(block, count, axes):
    return exchange(jnp.broadcast_to(block[None], (count,) + block.shape), axes)


def swap_cores(block):
    return lax.ppermute(block, "core", [(0, 1), (1, 0)])


def in_vmem(kernel, out_shape, operands, waits=()):
    vmem = pl.BlockSpec(memory_space=pltpu.VMEM)
    kept = pl.BlockSpec(memory_space=pl.ANY)
    return pl.pallas_call(
        kernel,
        out_shape=jax.ShapeDtypeStruct(out_shape, BF16),
        in_specs=[vmem] * len(operands) + [kept] * len(waits),
        out_specs=vmem,
        compiler_params=pltpu.CompilerParams(vmem_limit_bytes=32 << 20),
    )(*operands, *waits)


def first_products(got_ref, in_own, in_other, out_own, out_other, parts_ref):
    n_near, _, few, both = got_ref.shape
    width = both // CORES
    shape = (parts_ref.shape[0],) + parts_ref.shape[2:]
    rows = got_ref[:, 0].reshape(n_near * few, both)
    part = times(rows[:, :width], in_own[...]) + times(rows[:, width:], in_other[...])
    parts_ref[:, 0] = part.astype(BF16).reshape(shape)
    rows = got_ref[:, 1].reshape(n_near * few, both)
    part = times_transposed(rows[:, :width], out_own[...])
    part = part + times_transposed(rows[:, width:], out_other[...])
    parts_ref[:, 1] = part.astype(BF16).reshape(shape)


def second_products(rows_ref, in_own, in_other, out_own, out_other, *rest):
    parts_ref = rest[-1]
    n_z, _, few, hidden = rows_ref.shape
    width = in_own.shape[0]
    shape = (parts_ref.shape[0], parts_ref.shape[2], width)
    rows = rows_ref[:, 0].reshape(n_z * few, hidden)
    parts_ref[:, 0, :, :width] = times(rows, out_own[...]).astype(BF16).reshape(shape)
    parts_ref[:, 0, :, width:] = times(rows, out_other[...]).astype(BF16).reshape(shape)
    rows = rows_ref[:, 1].reshape(n_z * few, hidden)
    parts_ref[:, 1, :, :width] = times_transposed(rows, in_own[...]).astype(BF16).reshape(shape)
    parts_ref[:, 1, :, width:] = times_transposed(rows, in_other[...]).astype(BF16).reshape(shape)


def shards(n_z, n_near, n_far, activations, in_weight, out_weight, cotangent):
    tokens, width = activations.shape
    hidden = in_weight.shape[1]
    half = tokens // CORES
    few = n_far * half
    some = n_near * few
    first_core = lax.axis_index("core") == 0

    in_other = swap_cores(in_weight)
    out_other = swap_cores(out_weight)
    weights = (in_weight, in_other, out_weight, out_other)

    sent = jnp.stack([activations, cotangent]).reshape(2, CORES, half, width)
    sent = jnp.broadcast_to(sent.transpose(1, 0, 2, 3)[None], (n_far, CORES, 2, half, width))
    got = exchange(sent.reshape(n_far * CORES, 2, half, width), FAR)
    got = got.reshape(n_far, CORES, 2, half, width)
    got = jnp.where(first_core, got, got[:, ::-1]).transpose(2, 0, 3, 1, 4)
    got = to_all(got.reshape(2, few, CORES * width), n_near, NEAR)

    parts = in_vmem(first_products, (n_z, 2, some // n_z, hidden), (got,) + weights)
    sums = jnp.sum(exchange(parts, "z").astype(F32), axis=0)
    pre_act, act_grad = sums[0], sums[1]
    hidden_rows = gelu_value(pre_act).astype(BF16)
    pre_grad_rows = (act_grad * gelu_slope(pre_act)).astype(BF16)
    rows = to_all(jnp.stack([hidden_rows, pre_grad_rows]), n_z, "z")

    token_others = swap_cores(got[:, :, :, width:])
    parts = in_vmem(
        second_products, (n_near, 2, few, CORES * width), (rows,) + weights, (token_others,)
    )
    sums = jnp.sum(exchange(parts, NEAR).astype(F32), axis=0).astype(BF16)
    parts = sums.reshape(2, n_far, half, CORES, width)
    parts = jnp.where(first_core, parts, parts[:, :, :, ::-1]).transpose(1, 3, 0, 2, 4)
    parts = exchange(parts.reshape(n_far * CORES, 2, half, width), FAR)
    sums = jnp.sum(parts.reshape(n_far, CORES, 2, half, width).astype(F32), axis=0).astype(BF16)
    sums = sums.transpose(1, 0, 2, 3).reshape(2, tokens, width)

    def all_rows(blocks, which):
        return blocks[:, which].reshape(some, blocks.shape[3])

    token_owns = got[:, :, :, :width]
    row_others = swap_cores(rows)
    in_weight_gradient = (
        over_tokens(all_rows(token_owns, 0), all_rows(rows, 1))
        + over_tokens(all_rows(token_others, 0), all_rows(row_others, 1))
    ).astype(BF16)
    out_weight_gradient = (
        over_tokens(all_rows(rows, 0), all_rows(token_owns, 1))
        + over_tokens(all_rows(row_others, 0), all_rows(token_others, 1))
    ).astype(BF16)
    return sums[0], sums[1], in_weight_gradient, out_weight_gradient


def solution(mesh):
    n_z = mesh.shape["row"] // CORES
    n_x = mesh.shape["col"] // (Y_NEAR * Y_FAR)
    fine = Mesh(
        np.asarray(mesh.devices).reshape(n_z, CORES, n_x, Y_FAR, Y_NEAR),
        ("z", "core", "x", "yh", "yl"),
    )
    row, col = ("z", "core"), ("x", "yh", "yl")

    def part(*arrays):
        return shards(n_z, n_x * Y_NEAR, Y_FAR, *arrays)

    return jax.shard_map(
        part,
        mesh=fine,
        in_specs=(P(col, row), P(row, col), P(col, row), P(col, row)),
        out_specs=(P(col, row), P(col, row), P(row, col), P(col, row)),
        check_vma=False,
    )
```

```python
import math

import jax
import jax.numpy as jnp
import numpy as np
from jax import lax
from jax.experimental import pallas as pl
from jax.experimental.pallas import tpu as pltpu
from jax.sharding import Mesh, PartitionSpec as P

GELU_C = math.sqrt(2.0 / math.pi)
BF16 = jnp.bfloat16
F32 = jnp.float32

CORES = 2
Y_NEAR = 2
Y_FAR = 4
NEAR = ("x", "yl")
FAR = ("yh", "core")


def gelu_value(hidden):
    inner = GELU_C * (hidden + 0.044715 * hidden * hidden * hidden)
    return 0.5 * hidden * (1.0 + jnp.tanh(inner))


def gelu_slope(hidden):
    tanh_value = jnp.tanh(GELU_C * (hidden + 0.044715 * hidden * hidden * hidden))
    return 0.5 * (1.0 + tanh_value) + 0.5 * hidden * (1.0 - tanh_value * tanh_value) * GELU_C * (
        1.0 + 3.0 * 0.044715 * hidden * hidden
    )


def times(left_side, right_side):
    return jnp.dot(left_side, right_side, preferred_element_type=F32)


def times_transposed(left_side, right_side):
    return lax.dot_general(
        left_side, right_side, (((1,), (1,)), ((), ())), preferred_element_type=F32
    )


def over_tokens(left_side, right_side):
    return lax.dot_general(
        left_side, right_side, (((0,), (0,)), ((), ())), preferred_element_type=F32
    )


def exchange(blocks, axes):
    return lax.all_to_all(blocks, axes, 0, 0, tiled=True)


def to_all(block, count, axes):
    return exchange(jnp.broadcast_to(block[None], (count,) + block.shape), axes)


def swap_cores(block):
    return lax.ppermute(block, "core", [(0, 1), (1, 0)])


VMEM = pl.BlockSpec(memory_space=pltpu.VMEM)
HBM = pl.BlockSpec(memory_space=pltpu.HBM)


def with_weights(kernel, out_shape, rows, weights):
    flops = 8 * rows.shape[0] * rows.shape[2] * weights[0].shape[0] * weights[0].shape[1]
    return pl.pallas_call(
        kernel,
        out_shape=jax.ShapeDtypeStruct(out_shape, BF16),
        in_specs=[VMEM] + [HBM] * len(weights),
        out_specs=VMEM,
        scratch_shapes=[pltpu.VMEM(w.shape, w.dtype) for w in weights]
        + [pltpu.SemaphoreType.DMA((len(weights),))],
        cost_estimate=pl.CostEstimate(flops=flops, bytes_accessed=8 << 20, transcendentals=0),
        compiler_params=pltpu.CompilerParams(vmem_limit_bytes=24 << 20),
    )(rows, *weights)


def fetch(sources, targets, sems):
    copies = [
        pltpu.make_async_copy(source, target, sems.at[i])
        for i, (source, target) in enumerate(zip(sources, targets))
    ]
    for copy in copies:
        copy.start()
    return copies


def first_products(got_ref, i0, i1, o0, o1, parts_ref, in_own, in_other, out_own, out_other, sems):
    copies = fetch((i0, i1, o0, o1), (in_own, in_other, out_own, out_other), sems)
    n_near, _, few, both = got_ref.shape
    width = both // CORES
    shape = (parts_ref.shape[0],) + parts_ref.shape[2:]
    rows = got_ref[:, 0].reshape(n_near * few, both)
    copies[0].wait()
    part = times(rows[:, :width], in_own[...])
    copies[1].wait()
    part = part + times(rows[:, width:], in_other[...])
    parts_ref[:, 0] = part.astype(BF16).reshape(shape)
    rows = got_ref[:, 1].reshape(n_near * few, both)
    copies[2].wait()
    part = times_transposed(rows[:, :width], out_own[...])
    copies[3].wait()
    part = part + times_transposed(rows[:, width:], out_other[...])
    parts_ref[:, 1] = part.astype(BF16).reshape(shape)


def second_products(rows_ref, i0, i1, o0, o1, parts_ref, in_own, in_other, out_own, out_other, sems):
    copies = fetch((i0, i1, o0, o1), (in_own, in_other, out_own, out_other), sems)
    n_z, _, few, hidden = rows_ref.shape
    width = in_own.shape[0]
    shape = (parts_ref.shape[0], parts_ref.shape[2], width)
    rows = rows_ref[:, 1].reshape(n_z * few, hidden)
    copies[0].wait()
    parts_ref[:, 1, :, :width] = times_transposed(rows, in_own[...]).astype(BF16).reshape(shape)
    copies[1].wait()
    parts_ref[:, 1, :, width:] = times_transposed(rows, in_other[...]).astype(BF16).reshape(shape)
    rows = rows_ref[:, 0].reshape(n_z * few, hidden)
    copies[2].wait()
    parts_ref[:, 0, :, :width] = times(rows, out_own[...]).astype(BF16).reshape(shape)
    copies[3].wait()
    parts_ref[:, 0, :, width:] = times(rows, out_other[...]).astype(BF16).reshape(shape)


def gradients(got_ref, token_others_ref, rows_ref, row_others_ref, in_ref, out_ref):
    width = in_ref.shape[0]

    def flat(block):
        return block.reshape(block.shape[0] * block.shape[1], block.shape[2])

    part = over_tokens(flat(got_ref[:, 0, :, :width]), flat(rows_ref[:, 1]))
    part = part + over_tokens(flat(token_others_ref[:, 0]), flat(row_others_ref[:, 1]))
    in_ref[...] = part.astype(BF16)
    part = over_tokens(flat(rows_ref[:, 0]), flat(got_ref[:, 1, :, :width]))
    part = part + over_tokens(flat(row_others_ref[:, 0]), flat(token_others_ref[:, 1]))
    out_ref[...] = part.astype(BF16)


def shards(n_z, n_near, n_far, activations, in_weight, out_weight, cotangent):
    tokens, width = activations.shape
    hidden = in_weight.shape[1]
    half = tokens // CORES
    few = n_far * half
    some = n_near * few
    first_core = lax.axis_index("core") == 0

    in_other = swap_cores(in_weight)
    out_other = swap_cores(out_weight)
    weights = (in_weight, in_other, out_weight, out_other)

    sent = jnp.stack([activations, cotangent]).reshape(2, CORES, half, width)
    sent = jnp.broadcast_to(sent.transpose(1, 0, 2, 3)[None], (n_far, CORES, 2, half, width))
    got = exchange(sent.reshape(n_far * CORES, 2, half, width), FAR)
    got = got.reshape(n_far, CORES, 2, half, width)
    got = jnp.where(first_core, got, got[:, ::-1]).transpose(2, 0, 3, 1, 4)
    got = to_all(got.reshape(2, few, CORES * width), n_near, NEAR)

    parts = with_weights(first_products, (n_z, 2, some // n_z, hidden), got, weights)
    sums = jnp.sum(exchange(parts, "z").astype(F32), axis=0)
    pre_act, act_grad = sums[0], sums[1]
    hidden_rows = gelu_value(pre_act).astype(BF16)
    pre_grad_rows = (act_grad * gelu_slope(pre_act)).astype(BF16)
    rows = to_all(jnp.stack([hidden_rows, pre_grad_rows]), n_z, "z")

    parts = with_weights(second_products, (n_near, 2, few, CORES * width), rows, weights)
    sums = jnp.sum(exchange(parts, NEAR).astype(F32), axis=0).astype(BF16)
    own, other = sums[:, :, :width], sums[:, :, width:]
    parts = jnp.stack([jnp.where(first_core, own, other), jnp.where(first_core, other, own)])
    parts = parts.reshape(CORES, 2, n_far, half, width).transpose(2, 0, 1, 3, 4)
    parts = exchange(parts.reshape(n_far * CORES, 2, half, width), FAR)
    sums = jnp.sum(parts.reshape(n_far, CORES, 2, half, width).astype(F32), axis=0).astype(BF16)
    sums = sums.transpose(1, 0, 2, 3).reshape(2, tokens, width)

    token_others = swap_cores(got[:, :, :, width:])
    row_others = swap_cores(rows)
    in_weight_gradient, out_weight_gradient = pl.pallas_call(
        gradients,
        out_shape=[jax.ShapeDtypeStruct(w.shape, BF16) for w in (in_weight, out_weight)],
        in_specs=[VMEM] * 4,
        out_specs=[VMEM] * 2,
        cost_estimate=pl.CostEstimate(
            flops=8 * some * width * hidden, bytes_accessed=8 << 20, transcendentals=0
        ),
        compiler_params=pltpu.CompilerParams(vmem_limit_bytes=24 << 20),
    )(got, token_others, rows, row_others)
    return sums[0], sums[1], in_weight_gradient, out_weight_gradient


def solution(mesh):
    n_z = mesh.shape["row"] // CORES
    n_x = mesh.shape["col"] // (Y_NEAR * Y_FAR)
    fine = Mesh(
        np.asarray(mesh.devices).reshape(n_z, CORES, n_x, Y_FAR, Y_NEAR),
        ("z", "core", "x", "yh", "yl"),
    )
    row, col = ("z", "core"), ("x", "yh", "yl")

    def part(*arrays):
        return shards(n_z, n_x * Y_NEAR, Y_FAR, *arrays)

    return jax.shard_map(
        part,
        mesh=fine,
        in_specs=(P(col, row), P(row, col), P(col, row), P(col, row)),
        out_specs=(P(col, row), P(col, row), P(row, col), P(col, row)),
        check_vma=False,
    )
```

```python
import math

import jax
import jax.numpy as jnp
import numpy as np
from jax import lax
from jax.experimental import pallas as pl
from jax.experimental.pallas import tpu as pltpu
from jax.sharding import Mesh, PartitionSpec as P

GELU_C = math.sqrt(2.0 / math.pi)
BF16 = jnp.bfloat16
F32 = jnp.float32

CORES = 2
Y_NEAR = 2
Y_FAR = 4
NEAR = ("x", "yl")
FAR = ("yh", "core")


def gelu_value(hidden):
    inner = GELU_C * (hidden + 0.044715 * hidden * hidden * hidden)
    return 0.5 * hidden * (1.0 + jnp.tanh(inner))


def gelu_slope(hidden):
    tanh_value = jnp.tanh(GELU_C * (hidden + 0.044715 * hidden * hidden * hidden))
    return 0.5 * (1.0 + tanh_value) + 0.5 * hidden * (1.0 - tanh_value * tanh_value) * GELU_C * (
        1.0 + 3.0 * 0.044715 * hidden * hidden
    )


def times(left_side, right_side):
    return jnp.dot(left_side, right_side, preferred_element_type=F32)


def times_transposed(left_side, right_side):
    return lax.dot_general(
        left_side, right_side, (((1,), (1,)), ((), ())), preferred_element_type=F32
    )


def over_tokens(left_side, right_side):
    return lax.dot_general(
        left_side, right_side, (((0,), (0,)), ((), ())), preferred_element_type=F32
    )


def exchange(blocks, axes):
    return lax.all_to_all(blocks, axes, 0, 0, tiled=True)


def to_all(block, count, axes):
    return exchange(jnp.broadcast_to(block[None], (count,) + block.shape), axes)


def swap_cores(block):
    return lax.ppermute(block, "core", [(0, 1), (1, 0)])


VMEM = pl.BlockSpec(memory_space=pltpu.VMEM)
SMEM = pl.BlockSpec(memory_space=pltpu.SMEM)
KEPT = pl.BlockSpec(memory_space=pl.ANY)


def call(kernel, shapes, specs, operands, flops=0, scratch=()):
    shapes = [jax.ShapeDtypeStruct(shape, BF16) for shape in shapes]
    moved = 2 * (sum(x.size for x in operands) + sum(math.prod(x.shape) for x in shapes))
    results = pl.pallas_call(
        kernel,
        out_shape=shapes,
        in_specs=specs,
        out_specs=[VMEM] * len(shapes),
        scratch_shapes=scratch,
        cost_estimate=pl.CostEstimate(flops=flops, bytes_accessed=moved, transcendentals=0),
        compiler_params=pltpu.CompilerParams(vmem_limit_bytes=24 << 20),
    )(*operands)
    return results if len(shapes) > 1 else results[0]


def lay_out_tokens(activations_ref, cotangent_ref, sent_ref):
    half = activations_ref.shape[0] // CORES
    tokens = activations_ref[...].astype(F32)
    cotangent = cotangent_ref[...].astype(F32)
    for core in range(CORES):
        mine = slice(core * half, (core + 1) * half)
        block = jnp.concatenate([tokens[mine], cotangent[mine]], 0).astype(BF16)
        for far in range(sent_ref.shape[0] // CORES):
            sent_ref[far * CORES + core] = block


def lay_out_widths(core_ref, got_ref, sent_ref):
    half, width = got_ref.shape[1] // 2, got_ref.shape[2]
    n_far = got_ref.shape[0] // CORES
    for which in range(2):
        rows = slice(which * half, (which + 1) * half)
        both = [
            jnp.concatenate(
                [got_ref[far * CORES + core].astype(F32)[rows] for far in range(n_far)], 0
            )
            for core in range(CORES)
        ]
        first = core_ref[0] == 0
        own = jnp.where(first, both[0], both[1]).astype(BF16)
        other = jnp.where(first, both[1], both[0]).astype(BF16)
        for near in range(sent_ref.shape[0]):
            sent_ref[near, which, :, :width] = own
            sent_ref[near, which, :, width:] = other


def first_products(got_ref, *rest):
    weights, parts_ref, held, sems = rest[:4], rest[4], rest[5:9], rest[9]
    copies = [
        pltpu.make_async_copy(weight, place, sems.at[i])
        for i, (weight, place) in enumerate(zip(weights, held))
    ]
    for copy in copies:
        copy.start()
    in_own, in_other, out_own, out_other = held
    n_near, _, few, both = got_ref.shape
    width = both // CORES
    shape = (parts_ref.shape[0],) + parts_ref.shape[2:]
    rows = got_ref[:, 0].reshape(n_near * few, both)
    copies[0].wait()
    part = times(rows[:, :width], in_own[...])
    copies[1].wait()
    part = part + times(rows[:, width:], in_other[...])
    parts_ref[:, 0] = part.astype(BF16).reshape(shape)
    rows = got_ref[:, 1].reshape(n_near * few, both)
    copies[2].wait()
    part = times_transposed(rows[:, :width], out_own[...])
    copies[3].wait()
    part = part + times_transposed(rows[:, width:], out_other[...])
    parts_ref[:, 1] = part.astype(BF16).reshape(shape)


def second_products(rows_ref, in_own, in_other, out_own, out_other, parts_ref):
    n_z, _, few, hidden = rows_ref.shape
    width = in_own.shape[0]
    shape = (parts_ref.shape[0], parts_ref.shape[2], width)
    rows = rows_ref[:, 0].reshape(n_z * few, hidden)
    parts_ref[:, 0, :, :width] = times(rows, out_own[...]).astype(BF16).reshape(shape)
    parts_ref[:, 0, :, width:] = times(rows, out_other[...]).astype(BF16).reshape(shape)
    rows = rows_ref[:, 1].reshape(n_z * few, hidden)
    parts_ref[:, 1, :, :width] = times_transposed(rows, in_own[...]).astype(BF16).reshape(shape)
    parts_ref[:, 1, :, width:] = times_transposed(rows, in_other[...]).astype(BF16).reshape(shape)


def sum_near(core_ref, parts_ref, sent_ref):
    width, half = sent_ref.shape[2], sent_ref.shape[1] // 2
    sums = []
    for which in range(2):
        total = parts_ref[0, which].astype(F32)
        for near in range(1, parts_ref.shape[0]):
            total = total + parts_ref[near, which].astype(F32)
        sums.append(total)
    first = core_ref[0] == 0
    own = [total[:, :width] for total in sums]
    other = [total[:, width:] for total in sums]
    by_core = [
        [jnp.where(first, mine, theirs) for mine, theirs in zip(own, other)],
        [jnp.where(first, theirs, mine) for mine, theirs in zip(own, other)],
    ]
    for far in range(sent_ref.shape[0] // CORES):
        rows = slice(far * half, (far + 1) * half)
        for core in range(CORES):
            block = jnp.concatenate([total[rows] for total in by_core[core]], 0)
            sent_ref[far * CORES + core] = block.astype(BF16)


def sum_far(parts_ref, layer_ref, input_ref):
    half = parts_ref.shape[1] // 2
    sums = []
    for core in range(CORES):
        total = parts_ref[core].astype(F32)
        for far in range(1, parts_ref.shape[0] // CORES):
            total = total + parts_ref[far * CORES + core].astype(F32)
        sums.append(total)
    layer_ref[...] = jnp.concatenate([total[:half] for total in sums], 0).astype(BF16)
    input_ref[...] = jnp.concatenate([total[half:] for total in sums], 0).astype(BF16)


def gradients(got_ref, token_others_ref, rows_ref, row_others_ref, in_ref, out_ref):
    width = in_ref.shape[0]

    def flat(block):
        return block.reshape(block.shape[0] * block.shape[1], block.shape[2])

    part = over_tokens(flat(got_ref[:, 0, :, :width]), flat(rows_ref[:, 1]))
    part = part + over_tokens(flat(token_others_ref[:, 0]), flat(row_others_ref[:, 1]))
    in_ref[...] = part.astype(BF16)
    part = over_tokens(flat(rows_ref[:, 0]), flat(got_ref[:, 1, :, :width]))
    part = part + over_tokens(flat(row_others_ref[:, 0]), flat(token_others_ref[:, 1]))
    out_ref[...] = part.astype(BF16)


def shards(n_z, n_near, n_far, activations, in_weight, out_weight, cotangent):
    tokens, width = activations.shape
    hidden = in_weight.shape[1]
    few = n_far * tokens // CORES
    some = n_near * few
    flops = 8 * some * width * hidden
    core = lax.axis_index("core").astype(jnp.int32).reshape(1)

    weights = (in_weight, swap_cores(in_weight), out_weight, swap_cores(out_weight))

    far_shape = (n_far * CORES, tokens, width)
    sent = call(lay_out_tokens, [far_shape], [VMEM] * 2, (activations, cotangent))
    got = exchange(sent, FAR)
    near_shape = (n_near, 2, few, CORES * width)
    got = exchange(call(lay_out_widths, [near_shape], [SMEM, VMEM], (core, got)), NEAR)

    z_shape = (n_z, 2, some // n_z, hidden)
    in_hbm = tuple(pltpu.with_memory_space_constraint(w, pltpu.HBM) for w in weights)
    scratch = [pltpu.VMEM(w.shape, BF16) for w in weights] + [pltpu.SemaphoreType.DMA((4,))]
    parts = call(
        first_products, [z_shape], [VMEM] + [KEPT] * 4, (got,) + in_hbm, flops, scratch
    )
    sums = jnp.sum(exchange(parts, "z").astype(F32), axis=0)
    pre_act, act_grad = sums[0], sums[1]
    hidden_rows = gelu_value(pre_act).astype(BF16)
    pre_grad_rows = (act_grad * gelu_slope(pre_act)).astype(BF16)
    rows = to_all(jnp.stack([hidden_rows, pre_grad_rows]), n_z, "z")

    parts = call(second_products, [near_shape], [VMEM] * 5, (rows,) + weights, flops)
    parts = call(sum_near, [far_shape], [SMEM, VMEM], (core, exchange(parts, NEAR)))
    layer_output, input_gradient = call(
        sum_far, [(tokens, width)] * 2, [VMEM], (exchange(parts, FAR),)
    )

    token_others = swap_cores(got[:, :, :, width:])
    row_others = swap_cores(rows)
    in_weight_gradient, out_weight_gradient = call(
        gradients,
        [in_weight.shape, out_weight.shape],
        [VMEM] * 4,
        (got, token_others, rows, row_others),
        flops,
    )
    return layer_output, input_gradient, in_weight_gradient, out_weight_gradient


def solution(mesh):
    n_z = mesh.shape["row"] // CORES
    n_x = mesh.shape["col"] // (Y_NEAR * Y_FAR)
    fine = Mesh(
        np.asarray(mesh.devices).reshape(n_z, CORES, n_x, Y_FAR, Y_NEAR),
        ("z", "core", "x", "yh", "yl"),
    )
    row, col = ("z", "core"), ("x", "yh", "yl")

    def part(*arrays):
        return shards(n_z, n_x * Y_NEAR, Y_FAR, *arrays)

    return jax.shard_map(
        part,
        mesh=fine,
        in_specs=(P(col, row), P(row, col), P(col, row), P(col, row)),
        out_specs=(P(col, row), P(col, row), P(row, col), P(col, row)),
        check_vma=False,
    )
```

```python
import math

import jax
import jax.numpy as jnp
import numpy as np
from jax import lax
from jax.experimental import pallas as pl
from jax.experimental.pallas import tpu as pltpu
from jax.sharding import Mesh, PartitionSpec as P

GELU_C = math.sqrt(2.0 / math.pi)
BF16 = jnp.bfloat16
F32 = jnp.float32

CORES = 2
Y_NEAR = 2
Y_FAR = 4
NEAR = ("x", "yl")
FAR = ("yh", "core")


def gelu_value(hidden):
    inner = GELU_C * (hidden + 0.044715 * hidden * hidden * hidden)
    return 0.5 * hidden * (1.0 + jnp.tanh(inner))


def gelu_slope(hidden):
    tanh_value = jnp.tanh(GELU_C * (hidden + 0.044715 * hidden * hidden * hidden))
    return 0.5 * (1.0 + tanh_value) + 0.5 * hidden * (1.0 - tanh_value * tanh_value) * GELU_C * (
        1.0 + 3.0 * 0.044715 * hidden * hidden
    )


def times(left_side, right_side):
    return jnp.dot(left_side, right_side, preferred_element_type=F32)


def times_transposed(left_side, right_side):
    return lax.dot_general(
        left_side, right_side, (((1,), (1,)), ((), ())), preferred_element_type=F32
    )


def over_tokens(left_side, right_side):
    return lax.dot_general(
        left_side, right_side, (((0,), (0,)), ((), ())), preferred_element_type=F32
    )


def exchange(blocks, axes):
    return lax.all_to_all(blocks, axes, 0, 0, tiled=True)


def to_all(block, count, axes):
    return exchange(jnp.broadcast_to(block[None], (count,) + block.shape), axes)


def swap_cores(block):
    return lax.ppermute(block, "core", [(0, 1), (1, 0)])


VMEM = pl.BlockSpec(memory_space=pltpu.VMEM)
SMEM = pl.BlockSpec(memory_space=pltpu.SMEM)
KEPT = pl.BlockSpec(memory_space=pl.ANY)


def call(kernel, shapes, specs, operands, flops=0, scratch=()):
    shapes = [jax.ShapeDtypeStruct(shape, BF16) for shape in shapes]
    moved = 2 * (sum(x.size for x in operands) + sum(math.prod(x.shape) for x in shapes))
    results = pl.pallas_call(
        kernel,
        out_shape=shapes,
        in_specs=specs,
        out_specs=[VMEM] * len(shapes),
        scratch_shapes=scratch,
        cost_estimate=pl.CostEstimate(flops=flops, bytes_accessed=moved, transcendentals=0),
        compiler_params=pltpu.CompilerParams(vmem_limit_bytes=24 << 20),
    )(*operands)
    return results if len(shapes) > 1 else results[0]


def lay_out_tokens(activations_ref, cotangent_ref, sent_ref, here, sems):
    half = activations_ref.shape[0] // CORES
    first = pltpu.make_async_copy(activations_ref, here.at[0], sems.at[0])
    second = pltpu.make_async_copy(cotangent_ref, here.at[1], sems.at[1])
    first.start()
    second.start()
    first.wait()
    second.wait()
    tokens = here[0].astype(F32)
    cotangent = here[1].astype(F32)
    for core in range(CORES):
        mine = slice(core * half, (core + 1) * half)
        block = jnp.concatenate([tokens[mine], cotangent[mine]], 0).astype(BF16)
        for far in range(sent_ref.shape[0] // CORES):
            sent_ref[far * CORES + core] = block


def lay_out_widths(core_ref, got_ref, sent_ref):
    half, width = got_ref.shape[1] // 2, got_ref.shape[2]
    n_far = got_ref.shape[0] // CORES
    for which in range(2):
        rows = slice(which * half, (which + 1) * half)
        both = [
            jnp.concatenate(
                [got_ref[far * CORES + core].astype(F32)[rows] for far in range(n_far)], 0
            )
            for core in range(CORES)
        ]
        first = core_ref[0] == 0
        own = jnp.where(first, both[0], both[1]).astype(BF16)
        other = jnp.where(first, both[1], both[0]).astype(BF16)
        for near in range(sent_ref.shape[0]):
            sent_ref[near, which, :, :width] = own
            sent_ref[near, which, :, width:] = other


def first_products(got_ref, *rest):
    weights, parts_ref, held, sems = rest[:4], rest[4], rest[5:9], rest[9]
    copies = [
        pltpu.make_async_copy(weight, place, sems.at[i])
        for i, (weight, place) in enumerate(zip(weights, held))
    ]
    for copy in copies:
        copy.start()
    in_own, in_other, out_own, out_other = held
    n_near, _, few, both = got_ref.shape
    width = both // CORES
    shape = (parts_ref.shape[0],) + parts_ref.shape[2:]
    rows = got_ref[:, 0].reshape(n_near * few, both)
    copies[0].wait()
    part = times(rows[:, :width], in_own[...])
    copies[1].wait()
    part = part + times(rows[:, width:], in_other[...])
    parts_ref[:, 0] = part.astype(BF16).reshape(shape)
    rows = got_ref[:, 1].reshape(n_near * few, both)
    copies[2].wait()
    part = times_transposed(rows[:, :width], out_own[...])
    copies[3].wait()
    part = part + times_transposed(rows[:, width:], out_other[...])
    parts_ref[:, 1] = part.astype(BF16).reshape(shape)


def second_products(rows_ref, in_own, in_other, out_own, out_other, parts_ref):
    n_z, _, few, hidden = rows_ref.shape
    width = in_own.shape[0]
    shape = (parts_ref.shape[0], parts_ref.shape[2], width)
    rows = rows_ref[:, 0].reshape(n_z * few, hidden)
    parts_ref[:, 0, :, :width] = times(rows, out_own[...]).astype(BF16).reshape(shape)
    parts_ref[:, 0, :, width:] = times(rows, out_other[...]).astype(BF16).reshape(shape)
    rows = rows_ref[:, 1].reshape(n_z * few, hidden)
    parts_ref[:, 1, :, :width] = times_transposed(rows, in_own[...]).astype(BF16).reshape(shape)
    parts_ref[:, 1, :, width:] = times_transposed(rows, in_other[...]).astype(BF16).reshape(shape)


def sum_near(core_ref, parts_ref, sent_ref):
    width, half = sent_ref.shape[2], sent_ref.shape[1] // 2
    sums = []
    for which in range(2):
        total = parts_ref[0, which].astype(F32)
        for near in range(1, parts_ref.shape[0]):
            total = total + parts_ref[near, which].astype(F32)
        sums.append(total)
    first = core_ref[0] == 0
    own = [total[:, :width] for total in sums]
    other = [total[:, width:] for total in sums]
    by_core = [
        [jnp.where(first, mine, theirs) for mine, theirs in zip(own, other)],
        [jnp.where(first, theirs, mine) for mine, theirs in zip(own, other)],
    ]
    for far in range(sent_ref.shape[0] // CORES):
        rows = slice(far * half, (far + 1) * half)
        for core in range(CORES):
            block = jnp.concatenate([total[rows] for total in by_core[core]], 0)
            sent_ref[far * CORES + core] = block.astype(BF16)


def sum_far(parts_ref, layer_ref, input_ref):
    half = parts_ref.shape[1] // 2
    sums = []
    for core in range(CORES):
        total = parts_ref[core].astype(F32)
        for far in range(1, parts_ref.shape[0] // CORES):
            total = total + parts_ref[far * CORES + core].astype(F32)
        sums.append(total)
    layer_ref[...] = jnp.concatenate([total[:half] for total in sums], 0).astype(BF16)
    input_ref[...] = jnp.concatenate([total[half:] for total in sums], 0).astype(BF16)


def gradients(got_ref, token_others_ref, rows_ref, row_others_ref, in_ref, out_ref):
    width = in_ref.shape[0]

    def flat(block):
        return block.reshape(block.shape[0] * block.shape[1], block.shape[2])

    part = over_tokens(flat(got_ref[:, 0, :, :width]), flat(rows_ref[:, 1]))
    part = part + over_tokens(flat(token_others_ref[:, 0]), flat(row_others_ref[:, 1]))
    in_ref[...] = part.astype(BF16)
    part = over_tokens(flat(rows_ref[:, 0]), flat(got_ref[:, 1, :, :width]))
    part = part + over_tokens(flat(row_others_ref[:, 0]), flat(token_others_ref[:, 1]))
    out_ref[...] = part.astype(BF16)


def shards(n_z, n_near, n_far, activations, in_weight, out_weight, cotangent):
    tokens, width = activations.shape
    hidden = in_weight.shape[1]
    few = n_far * tokens // CORES
    some = n_near * few
    flops = 8 * some * width * hidden
    core = lax.axis_index("core").astype(jnp.int32).reshape(1)

    weights = (in_weight, swap_cores(in_weight), out_weight, swap_cores(out_weight))

    far_shape = (n_far * CORES, tokens, width)
    scratch = [pltpu.VMEM((2, tokens, width), BF16), pltpu.SemaphoreType.DMA((2,))]
    in_hbm = [pltpu.with_memory_space_constraint(x, pltpu.HBM) for x in (activations, cotangent)]
    sent = call(lay_out_tokens, [far_shape], [KEPT] * 2, in_hbm, 0, scratch)
    got = exchange(sent, FAR)
    near_shape = (n_near, 2, few, CORES * width)
    got = exchange(call(lay_out_widths, [near_shape], [SMEM, VMEM], (core, got)), NEAR)

    z_shape = (n_z, 2, some // n_z, hidden)
    in_hbm = tuple(pltpu.with_memory_space_constraint(w, pltpu.HBM) for w in weights)
    parts, *held = call(
        first_products,
        [z_shape] + [w.shape for w in weights],
        [VMEM] + [KEPT] * 4,
        (got,) + in_hbm,
        flops,
        [pltpu.SemaphoreType.DMA((4,))],
    )
    sums = jnp.sum(exchange(parts, "z").astype(F32), axis=0)
    pre_act, act_grad = sums[0], sums[1]
    hidden_rows = gelu_value(pre_act).astype(BF16)
    pre_grad_rows = (act_grad * gelu_slope(pre_act)).astype(BF16)
    rows = to_all(jnp.stack([hidden_rows, pre_grad_rows]), n_z, "z")

    parts = call(second_products, [near_shape], [VMEM] * 5, (rows, *held), flops)
    parts = call(sum_near, [far_shape], [SMEM, VMEM], (core, exchange(parts, NEAR)))
    layer_output, input_gradient = call(
        sum_far, [(tokens, width)] * 2, [VMEM], (exchange(parts, FAR),)
    )

    token_others = swap_cores(got[:, :, :, width:])
    row_others = swap_cores(rows)
    in_weight_gradient, out_weight_gradient = call(
        gradients,
        [in_weight.shape, out_weight.shape],
        [VMEM] * 4,
        (got, token_others, rows, row_others),
        flops,
    )
    return layer_output, input_gradient, in_weight_gradient, out_weight_gradient


def solution(mesh):
    n_z = mesh.shape["row"] // CORES
    n_x = mesh.shape["col"] // (Y_NEAR * Y_FAR)
    fine = Mesh(
        np.asarray(mesh.devices).reshape(n_z, CORES, n_x, Y_FAR, Y_NEAR),
        ("z", "core", "x", "yh", "yl"),
    )
    row, col = ("z", "core"), ("x", "yh", "yl")

    def part(*arrays):
        return shards(n_z, n_x * Y_NEAR, Y_FAR, *arrays)

    return jax.shard_map(
        part,
        mesh=fine,
        in_specs=(P(col, row), P(row, col), P(col, row), P(col, row)),
        out_specs=(P(col, row), P(col, row), P(row, col), P(col, row)),
        check_vma=False,
    )
```

```python
import math

import jax
import jax.numpy as jnp
import numpy as np
from jax import lax
from jax.experimental import pallas as pl
from jax.experimental.pallas import tpu as pltpu
from jax.sharding import Mesh, PartitionSpec as P

GELU_C = math.sqrt(2.0 / math.pi)
BF16 = jnp.bfloat16
F32 = jnp.float32

CORES = 2
Y_NEAR = 2
Y_FAR = 4
NEAR = ("x", "yl")
FAR = ("yh", "core")


def gelu_value(hidden):
    inner = GELU_C * (hidden + 0.044715 * hidden * hidden * hidden)
    return 0.5 * hidden * (1.0 + jnp.tanh(inner))


def gelu_slope(hidden):
    tanh_value = jnp.tanh(GELU_C * (hidden + 0.044715 * hidden * hidden * hidden))
    return 0.5 * (1.0 + tanh_value) + 0.5 * hidden * (1.0 - tanh_value * tanh_value) * GELU_C * (
        1.0 + 3.0 * 0.044715 * hidden * hidden
    )


def times(left_side, right_side):
    return jnp.dot(left_side, right_side, preferred_element_type=F32)


def times_transposed(left_side, right_side):
    return lax.dot_general(
        left_side, right_side, (((1,), (1,)), ((), ())), preferred_element_type=F32
    )


def over_tokens(left_side, right_side):
    return lax.dot_general(
        left_side, right_side, (((0,), (0,)), ((), ())), preferred_element_type=F32
    )


def exchange(blocks, axes):
    rows = blocks.reshape(blocks.shape[0], -1, blocks.shape[-1])
    return lax.all_to_all(rows, axes, 0, 0, tiled=True).reshape(blocks.shape)


def to_all(block, count, axes):
    return exchange(jnp.broadcast_to(block[None], (count,) + block.shape), axes)


def swap_cores(block):
    return lax.ppermute(block, "core", [(0, 1), (1, 0)])


VMEM = pl.BlockSpec(memory_space=pltpu.VMEM)
SMEM = pl.BlockSpec(memory_space=pltpu.SMEM)
KEPT = pl.BlockSpec(memory_space=pl.ANY)


def call(kernel, shapes, specs, operands, flops=0, scratch=(), to_hbm=False):
    specs_out = [KEPT if to_hbm else VMEM] * len(shapes)
    place = pltpu.HBM if to_hbm else jax.ShapeDtypeStruct
    shapes = [place(shape, BF16) for shape in shapes]
    moved = 2 * (sum(x.size for x in operands) + sum(math.prod(x.shape) for x in shapes))
    results = pl.pallas_call(
        kernel,
        out_shape=shapes,
        in_specs=specs,
        out_specs=specs_out,
        scratch_shapes=scratch,
        cost_estimate=pl.CostEstimate(flops=flops, bytes_accessed=moved, transcendentals=0),
        compiler_params=pltpu.CompilerParams(vmem_limit_bytes=24 << 20),
    )(*operands)
    return results if len(shapes) > 1 else results[0]


def lay_out_tokens(activations_ref, cotangent_ref, sent_ref, here, sems):
    half = activations_ref.shape[0] // CORES
    first = pltpu.make_async_copy(activations_ref, here.at[0], sems.at[0])
    second = pltpu.make_async_copy(cotangent_ref, here.at[1], sems.at[1])
    first.start()
    second.start()
    first.wait()
    second.wait()
    tokens = here[0].astype(F32)
    cotangent = here[1].astype(F32)
    for core in range(CORES):
        mine = slice(core * half, (core + 1) * half)
        block = jnp.concatenate([tokens[mine], cotangent[mine]], 0).astype(BF16)
        for far in range(sent_ref.shape[0] // CORES):
            sent_ref[far * CORES + core] = block


def lay_out_widths(core_ref, got_ref, *rest):
    sent_ref = rest[-1]
    half = got_ref.shape[1] // 2
    n_far = got_ref.shape[0] // CORES
    for which in range(2):
        rows = slice(which * half, (which + 1) * half)
        both = [
            jnp.concatenate(
                [got_ref[far * CORES + core].astype(F32)[rows] for far in range(n_far)], 0
            )
            for core in range(CORES)
        ]
        first = core_ref[0] == 0
        own = jnp.where(first, both[0], both[1]).astype(BF16)
        other = jnp.where(first, both[1], both[0]).astype(BF16)
        for near in range(sent_ref.shape[0]):
            sent_ref[near, which, 0] = own
            sent_ref[near, which, 1] = other


def flat(block):
    return block.reshape(block.shape[0] * block.shape[1], block.shape[2])


def first_products(got_ref, in_own, in_other, out_own, out_other, parts_ref):
    shape = (parts_ref.shape[0],) + parts_ref.shape[2:]
    part = times(flat(got_ref[:, 0, 0]), in_own[...])
    part = part + times(flat(got_ref[:, 0, 1]), in_other[...])
    parts_ref[:, 0] = part.astype(BF16).reshape(shape)
    part = times_transposed(flat(got_ref[:, 1, 0]), out_own[...])
    part = part + times_transposed(flat(got_ref[:, 1, 1]), out_other[...])
    parts_ref[:, 1] = part.astype(BF16).reshape(shape)


def second_products(rows_ref, in_own, in_other, out_own, out_other, parts_ref, made, sems):
    shape = (made.shape[0],) + made.shape[3:]
    copies = []
    for which, product, weights in (
        (0, times, (out_own, out_other)),
        (1, times_transposed, (in_own, in_other)),
    ):
        rows = flat(rows_ref[:, which])
        for i, weight in enumerate(weights):
            made[:, which, i] = product(rows, weight[...]).astype(BF16).reshape(shape)
            copies.append(
                pltpu.make_async_copy(
                    made.at[:, which, i], parts_ref.at[:, which, i], sems.at[which, i]
                )
            )
            copies[-1].start()
    for copy in copies:
        copy.wait()


def sum_near(core_ref, parts_ref, sent_ref):
    half = sent_ref.shape[1] // 2

    def total(which, place):
        result = parts_ref[0, which, place].astype(F32)
        for near in range(1, parts_ref.shape[0]):
            result = result + parts_ref[near, which, place].astype(F32)
        return result

    own = [total(which, 0) for which in range(2)]
    other = [total(which, 1) for which in range(2)]
    first = core_ref[0] == 0
    by_core = [
        [jnp.where(first, mine, theirs) for mine, theirs in zip(own, other)],
        [jnp.where(first, theirs, mine) for mine, theirs in zip(own, other)],
    ]
    for far in range(sent_ref.shape[0] // CORES):
        rows = slice(far * half, (far + 1) * half)
        for core in range(CORES):
            block = jnp.concatenate([sums[rows] for sums in by_core[core]], 0)
            sent_ref[far * CORES + core] = block.astype(BF16)


def sum_far(parts_ref, layer_ref, input_ref):
    half = parts_ref.shape[1] // 2
    sums = []
    for core in range(CORES):
        total = parts_ref[core].astype(F32)
        for far in range(1, parts_ref.shape[0] // CORES):
            total = total + parts_ref[far * CORES + core].astype(F32)
        sums.append(total)
    layer_ref[...] = jnp.concatenate([total[:half] for total in sums], 0).astype(BF16)
    input_ref[...] = jnp.concatenate([total[half:] for total in sums], 0).astype(BF16)


def gradients(got_ref, token_others_ref, rows_ref, row_others_ref, in_ref, out_ref):
    part = over_tokens(flat(got_ref[:, 0, 0]), flat(rows_ref[:, 1]))
    part = part + over_tokens(flat(token_others_ref[:, 0]), flat(row_others_ref[:, 1]))
    in_ref[...] = part.astype(BF16)
    part = over_tokens(flat(rows_ref[:, 0]), flat(got_ref[:, 1, 0]))
    part = part + over_tokens(flat(row_others_ref[:, 0]), flat(token_others_ref[:, 1]))
    out_ref[...] = part.astype(BF16)


def shards(n_z, n_near, n_far, activations, in_weight, out_weight, cotangent):
    tokens, width = activations.shape
    hidden = in_weight.shape[1]
    few = n_far * tokens // CORES
    some = n_near * few
    flops = 8 * some * width * hidden
    core = lax.axis_index("core").astype(jnp.int32).reshape(1)

    weights = (in_weight, swap_cores(in_weight), out_weight, swap_cores(out_weight))

    far_shape = (n_far * CORES, tokens, width)
    scratch = [pltpu.VMEM((2, tokens, width), BF16), pltpu.SemaphoreType.DMA((2,))]
    in_hbm = [pltpu.with_memory_space_constraint(x, pltpu.HBM) for x in (activations, cotangent)]
    sent = call(lay_out_tokens, [far_shape], [KEPT] * 2, in_hbm, 0, scratch)
    got = exchange(sent, FAR)
    near_shape = (n_near, 2, CORES, few, width)
    sent = call(
        lay_out_widths,
        [near_shape],
        [SMEM, VMEM, KEPT, KEPT],
        (core, got, weights[1], weights[3]),
    )
    got = exchange(sent, NEAR)

    z_shape = (n_z, 2, some // n_z, hidden)
    parts = call(first_products, [z_shape], [VMEM] * 5, (got, *weights), flops)
    sums = jnp.sum(exchange(parts, "z").astype(F32), axis=0)
    pre_act, act_grad = sums[0], sums[1]
    hidden_rows = gelu_value(pre_act).astype(BF16)
    pre_grad_rows = (act_grad * gelu_slope(pre_act)).astype(BF16)
    rows = to_all(jnp.stack([hidden_rows, pre_grad_rows]), n_z, "z")

    scratch = [pltpu.VMEM(near_shape, BF16), pltpu.SemaphoreType.DMA((2, CORES))]
    parts = call(
        second_products, [near_shape], [VMEM] * 5, (rows, *weights), flops, scratch, True
    )
    parts = call(sum_near, [far_shape], [SMEM, VMEM], (core, exchange(parts, NEAR)))
    layer_output, input_gradient = call(
        sum_far, [(tokens, width)] * 2, [VMEM], (exchange(parts, FAR),)
    )

    token_others = swap_cores(got[:, :, 1])
    row_others = swap_cores(rows)
    in_weight_gradient, out_weight_gradient = call(
        gradients,
        [in_weight.shape, out_weight.shape],
        [VMEM] * 4,
        (got, token_others, rows, row_others),
        flops,
    )
    return layer_output, input_gradient, in_weight_gradient, out_weight_gradient


def solution(mesh):
    n_z = mesh.shape["row"] // CORES
    n_x = mesh.shape["col"] // (Y_NEAR * Y_FAR)
    fine = Mesh(
        np.asarray(mesh.devices).reshape(n_z, CORES, n_x, Y_FAR, Y_NEAR),
        ("z", "core", "x", "yh", "yl"),
    )
    row, col = ("z", "core"), ("x", "yh", "yl")

    def part(*arrays):
        return shards(n_z, n_x * Y_NEAR, Y_FAR, *arrays)

    return jax.shard_map(
        part,
        mesh=fine,
        in_specs=(P(col, row), P(row, col), P(col, row), P(col, row)),
        out_specs=(P(col, row), P(col, row), P(row, col), P(col, row)),
        check_vma=False,
    )
```

```python
import math

import jax
import jax.numpy as jnp
import numpy as np
from jax import lax
from jax.experimental import pallas as pl
from jax.experimental.pallas import tpu as pltpu
from jax.sharding import Mesh, PartitionSpec as P

GELU_C = math.sqrt(2.0 / math.pi)
BF16 = jnp.bfloat16
F32 = jnp.float32

CORES = 2
Y_NEAR = 2
Y_FAR = 4
NEAR = ("x", "yl")
FAR = ("yh", "core")


def gelu_value(hidden):
    inner = GELU_C * (hidden + 0.044715 * hidden * hidden * hidden)
    return 0.5 * hidden * (1.0 + jnp.tanh(inner))


def gelu_slope(hidden):
    tanh_value = jnp.tanh(GELU_C * (hidden + 0.044715 * hidden * hidden * hidden))
    return 0.5 * (1.0 + tanh_value) + 0.5 * hidden * (1.0 - tanh_value * tanh_value) * GELU_C * (
        1.0 + 3.0 * 0.044715 * hidden * hidden
    )


def times(left_side, right_side):
    return jnp.dot(left_side, right_side, preferred_element_type=F32)


def times_transposed(left_side, right_side):
    return lax.dot_general(
        left_side, right_side, (((1,), (1,)), ((), ())), preferred_element_type=F32
    )


def over_tokens(left_side, right_side):
    return lax.dot_general(
        left_side, right_side, (((0,), (0,)), ((), ())), preferred_element_type=F32
    )


def exchange(blocks, axes):
    rows = blocks.reshape(blocks.shape[0], -1, blocks.shape[-1])
    return lax.all_to_all(rows, axes, 0, 0, tiled=True).reshape(blocks.shape)


def to_all(block, count, axes):
    return exchange(jnp.broadcast_to(block[None], (count,) + block.shape), axes)


def swap_cores(block):
    return lax.ppermute(block, "core", [(0, 1), (1, 0)])


VMEM = pl.BlockSpec(memory_space=pltpu.VMEM)
SMEM = pl.BlockSpec(memory_space=pltpu.SMEM)
KEPT = pl.BlockSpec(memory_space=pl.ANY)


def call(kernel, shapes, specs, operands, flops=0, scratch=(), to_hbm=False):
    specs_out = [KEPT if to_hbm else VMEM] * len(shapes)
    place = pltpu.HBM if to_hbm else jax.ShapeDtypeStruct
    shapes = [place(shape, BF16) for shape in shapes]
    moved = 2 * (sum(x.size for x in operands) + sum(math.prod(x.shape) for x in shapes))
    results = pl.pallas_call(
        kernel,
        out_shape=shapes,
        in_specs=specs,
        out_specs=specs_out,
        scratch_shapes=scratch,
        cost_estimate=pl.CostEstimate(flops=flops, bytes_accessed=moved, transcendentals=0),
        compiler_params=pltpu.CompilerParams(vmem_limit_bytes=24 << 20),
    )(*operands)
    return results if len(shapes) > 1 else results[0]


def lay_out_tokens(activations_ref, cotangent_ref, sent_ref, here, sems):
    half = activations_ref.shape[0] // CORES
    first = pltpu.make_async_copy(activations_ref, here.at[0], sems.at[0])
    second = pltpu.make_async_copy(cotangent_ref, here.at[1], sems.at[1])
    first.start()
    second.start()
    first.wait()
    second.wait()
    tokens = here[0].astype(F32)
    cotangent = here[1].astype(F32)
    for core in range(CORES):
        mine = slice(core * half, (core + 1) * half)
        block = jnp.concatenate([tokens[mine], cotangent[mine]], 0).astype(BF16)
        for far in range(sent_ref.shape[0] // CORES):
            sent_ref[far * CORES + core] = block


def lay_out_widths(core_ref, got_ref, *rest):
    sent_ref = rest[-1]
    half = got_ref.shape[1] // 2
    n_far = got_ref.shape[0] // CORES
    for which in range(2):
        rows = slice(which * half, (which + 1) * half)
        both = [
            jnp.concatenate(
                [got_ref[far * CORES + core].astype(F32)[rows] for far in range(n_far)], 0
            )
            for core in range(CORES)
        ]
        first = core_ref[0] == 0
        own = jnp.where(first, both[0], both[1]).astype(BF16)
        other = jnp.where(first, both[1], both[0]).astype(BF16)
        for near in range(sent_ref.shape[0]):
            sent_ref[near, which, 0] = own
            sent_ref[near, which, 1] = other


def flat(block):
    return block.reshape(block.shape[0] * block.shape[1], block.shape[2])


def hold(weight_ref, held_ref, sem):
    copy = pltpu.make_async_copy(weight_ref, held_ref, sem)
    copy.start()
    copy.wait()


def first_products(got_ref, in_own, in_other, out_own, out_other, parts_ref):
    shape = (parts_ref.shape[0],) + parts_ref.shape[2:]
    part = times(flat(got_ref[:, 0, 0]), in_own[...])
    part = part + times(flat(got_ref[:, 0, 1]), in_other[...])
    parts_ref[:, 0] = part.astype(BF16).reshape(shape)
    part = times_transposed(flat(got_ref[:, 1, 0]), out_own[...])
    part = part + times_transposed(flat(got_ref[:, 1, 1]), out_other[...])
    parts_ref[:, 1] = part.astype(BF16).reshape(shape)


def second_products(rows_ref, in_own, in_other, out_own, out_other, parts_ref, made, sems):
    shape = (made.shape[0],) + made.shape[3:]
    copies = []
    for which, product, weights in (
        (0, times, (out_own, out_other)),
        (1, times_transposed, (in_own, in_other)),
    ):
        rows = flat(rows_ref[:, which])
        for i, weight in enumerate(weights):
            made[:, which, i] = product(rows, weight[...]).astype(BF16).reshape(shape)
            copies.append(
                pltpu.make_async_copy(
                    made.at[:, which, i], parts_ref.at[:, which, i], sems.at[which, i]
                )
            )
            copies[-1].start()
    for copy in copies:
        copy.wait()


def sum_near(core_ref, parts_ref, sent_ref):
    half = sent_ref.shape[1] // 2

    def total(which, place):
        result = parts_ref[0, which, place].astype(F32)
        for near in range(1, parts_ref.shape[0]):
            result = result + parts_ref[near, which, place].astype(F32)
        return result

    own = [total(which, 0) for which in range(2)]
    other = [total(which, 1) for which in range(2)]
    first = core_ref[0] == 0
    by_core = [
        [jnp.where(first, mine, theirs) for mine, theirs in zip(own, other)],
        [jnp.where(first, theirs, mine) for mine, theirs in zip(own, other)],
    ]
    for far in range(sent_ref.shape[0] // CORES):
        rows = slice(far * half, (far + 1) * half)
        for core in range(CORES):
            block = jnp.concatenate([sums[rows] for sums in by_core[core]], 0)
            sent_ref[far * CORES + core] = block.astype(BF16)


def sum_far(parts_ref, layer_ref, input_ref):
    half = parts_ref.shape[1] // 2
    sums = []
    for core in range(CORES):
        total = parts_ref[core].astype(F32)
        for far in range(1, parts_ref.shape[0] // CORES):
            total = total + parts_ref[far * CORES + core].astype(F32)
        sums.append(total)
    layer_ref[...] = jnp.concatenate([total[:half] for total in sums], 0).astype(BF16)
    input_ref[...] = jnp.concatenate([total[half:] for total in sums], 0).astype(BF16)


def gradients(got_ref, token_others_ref, rows_ref, row_others_ref, in_ref, out_ref):
    part = over_tokens(flat(got_ref[:, 0, 0]), flat(rows_ref[:, 1]))
    part = part + over_tokens(flat(token_others_ref[:, 0]), flat(row_others_ref[:, 1]))
    in_ref[...] = part.astype(BF16)
    part = over_tokens(flat(rows_ref[:, 0]), flat(got_ref[:, 1, 0]))
    part = part + over_tokens(flat(row_others_ref[:, 0]), flat(token_others_ref[:, 1]))
    out_ref[...] = part.astype(BF16)


def shards(n_z, n_near, n_far, activations, in_weight, out_weight, cotangent):
    tokens, width = activations.shape
    hidden = in_weight.shape[1]
    few = n_far * tokens // CORES
    some = n_near * few
    flops = 8 * some * width * hidden
    core = lax.axis_index("core").astype(jnp.int32).reshape(1)

    in_own = call(
        hold,
        [in_weight.shape],
        [KEPT],
        [pltpu.with_memory_space_constraint(in_weight, pltpu.HBM)],
        20 * flops,
        [pltpu.SemaphoreType.DMA],
    )
    weights = (in_own, swap_cores(in_weight), out_weight, swap_cores(out_weight))

    far_shape = (n_far * CORES, tokens, width)
    scratch = [pltpu.VMEM((2, tokens, width), BF16), pltpu.SemaphoreType.DMA((2,))]
    in_hbm = [pltpu.with_memory_space_constraint(x, pltpu.HBM) for x in (activations, cotangent)]
    sent = call(lay_out_tokens, [far_shape], [KEPT] * 2, in_hbm, 0, scratch)
    got = exchange(sent, FAR)
    near_shape = (n_near, 2, CORES, few, width)
    sent = call(
        lay_out_widths,
        [near_shape],
        [SMEM, VMEM] + [KEPT] * 3,
        (core, got, in_own, weights[1], weights[3]),
    )
    got = exchange(sent, NEAR)

    z_shape = (n_z, 2, some // n_z, hidden)
    parts = call(first_products, [z_shape], [VMEM] * 5, (got, *weights), flops)
    sums = jnp.sum(exchange(parts, "z").astype(F32), axis=0)
    pre_act, act_grad = sums[0], sums[1]
    hidden_rows = gelu_value(pre_act).astype(BF16)
    pre_grad_rows = (act_grad * gelu_slope(pre_act)).astype(BF16)
    rows = to_all(jnp.stack([hidden_rows, pre_grad_rows]), n_z, "z")

    scratch = [pltpu.VMEM(near_shape, BF16), pltpu.SemaphoreType.DMA((2, CORES))]
    parts = call(
        second_products, [near_shape], [VMEM] * 5, (rows, *weights), flops, scratch, True
    )
    parts = call(sum_near, [far_shape], [SMEM, VMEM], (core, exchange(parts, NEAR)))
    layer_output, input_gradient = call(
        sum_far, [(tokens, width)] * 2, [VMEM], (exchange(parts, FAR),)
    )

    token_others = swap_cores(got[:, :, 1])
    row_others = swap_cores(rows)
    in_weight_gradient, out_weight_gradient = call(
        gradients,
        [in_weight.shape, out_weight.shape],
        [VMEM] * 4,
        (got, token_others, rows, row_others),
        flops,
    )
    return layer_output, input_gradient, in_weight_gradient, out_weight_gradient


def solution(mesh):
    n_z = mesh.shape["row"] // CORES
    n_x = mesh.shape["col"] // (Y_NEAR * Y_FAR)
    fine = Mesh(
        np.asarray(mesh.devices).reshape(n_z, CORES, n_x, Y_FAR, Y_NEAR),
        ("z", "core", "x", "yh", "yl"),
    )
    row, col = ("z", "core"), ("x", "yh", "yl")

    def part(*arrays):
        return shards(n_z, n_x * Y_NEAR, Y_FAR, *arrays)

    return jax.shard_map(
        part,
        mesh=fine,
        in_specs=(P(col, row), P(row, col), P(col, row), P(col, row)),
        out_specs=(P(col, row), P(col, row), P(row, col), P(col, row)),
        check_vma=False,
    )
```
